512 devices in a mesh: dp: 16 (over x, y), expert: 32 (over z, core).
Axes of the slice: x: 4, y: 4, z: 16, core: 2. Of those that a mesh axis runs over, the one named last changes fastest.
Arguments:
- queries: bfloat16 [65536, 2048], P(('dp', 'expert')), may hold values from -8 to 8
- key_value: bfloat16 [65536, 2, 2048], P(('dp', 'expert')), may hold values from -20 to 20
- memory: bfloat16 [512, 128, 2, 2048], P(('dp', 'expert')), may hold values from -6 to 6
- memory_source: int32 [512], P(('dp', 'expert')), may hold values from 0 to 1
- routing: int32 [65536, 1], P(('dp', 'expert')), may hold values from 0 to 63; in each aligned block of 128 rows (0 to 127, 128 to 255, ...) at most 3 rows name the same one
- router_weight: float32 [65536, 1], P(('dp', 'expert')), may hold values from 0.25 to 1
- norm_gain: float32 [2048], replicated, may hold values from 0.25 to 1.75
- gate_matrix: bfloat16 [2048, 90112], P(None, ('dp', 'expert')), may hold values from -0.125 to 0.125
- up_matrix: bfloat16 [2048, 90112], P(None, ('dp', 'expert')), may hold values from -0.125 to 0.125
- down_matrix: bfloat16 [90112, 2048], P(('dp', 'expert')), may hold values from -0.15625 to 0.15625
Outputs:
- layer_out: bfloat16 [65536, 2048], P(('dp', 'expert'))
The draws below stay inside these ranges and needn't reach their ends.
Inputs may be any that keep to these rules, and one draw needn't show every extreme that they name: `routing`: no expert is named by more than 3 tokens of one device; some expert is named by exactly 3 tokens of some device. A device's memory block is kept by the device 1 + memory_source places before it along dp, cyclically, with the same expert index.
All inputs are finite; a program needn't handle non-finite values.
Results may differ from the reference program's by a relative error of at most 0.023.
Values may be sent and summed in bfloat16 or wider, within the bound.
No kernel may reach another device: no remote copies, remote signals or barrier semaphores. Data moves between devices by JAX's collectives and lax.ppermute only.
A program may use at most 64 MiB of HBM per device.

```python
import math
import jax
import jax.numpy as jnp
import numpy as np
from jax import lax

D = 2048
FF = 1408
HEADS = 16
SLICES = 8
TOPK = 1
MEMLEN = 128
TOK_DEV = 128
EXPERTS = 64
MOST = 3
TOKENS = 65536
N_DP = 16
N_EXPERT = 32


def draw_queries(key, part):
    sampled = jnp.clip(jax.random.normal(jax.random.fold_in(key, 11), (TOKENS, D), jnp.float32), -6.0, 6.0)
    return sampled.astype(jnp.bfloat16)


def draw_key_value(key, part):
    sampled = jnp.clip(jax.random.normal(jax.random.fold_in(key, 12), (TOKENS, 2, D), jnp.float32), -6.0, 6.0)
    return sampled.astype(jnp.bfloat16)


def touch_ends(array, stream_key, low, top_value):
    longest = array.shape.index(max(array.shape))
    spots = []
    for shift in (0, 1):
        where = [jax.random.randint(jax.random.fold_in(stream_key, axis), (), 0, length) for axis, length in enumerate(array.shape)]
        where[longest] = (where[longest] + shift) % array.shape[longest]
        spots.append(tuple(where))
    return array.at[spots[0]].set(low).at[spots[1]].set(top_value)


def steps_of(own_key, extent, pieces, low, largest):
    def one(dim, shards_of):
        heights = jax.random.uniform(jax.random.fold_in(jax.random.fold_in(own_key, 6), dim), (shards_of,), jnp.float32, low / len(pieces), largest / len(pieces))
        return jnp.repeat(jnp.exp(heights), extent[dim] // shards_of).reshape((-1,) + (1,) * (len(extent) - dim - 1))

    gain = one(*pieces[0])
    for cut in pieces[1:]:
        gain = gain * one(*cut)
    return gain


def shared_out(rng, own, number, rows, amount, top, bound, slope):
    ranking = jax.random.permutation(rng, amount)
    heavy_load, common = shares(amount, rows * top, bound, slope, True), shares(amount, rows * top, bound, slope, False)
    places = jnp.arange(amount)

    def named(lengths, turn):
        used = int((lengths > 0).sum())
        fixed = max(1, used // 4)
        shifted = fixed + (places - fixed + turn * (used - fixed)) % max(1, amount - fixed)
        return jnp.zeros((amount,), jnp.int32).at[ranking[jnp.where(places < fixed, places, shifted)]].set(jnp.asarray(lengths, jnp.int32))

    lengths = jnp.where(number % 4 == 0, named(heavy_load, number // 4), named(common, number - number // 4 - 1))
    mixed = jax.random.permutation(jax.random.fold_in(own, 3), amount)
    giver, taker = mixed[0:amount // 2 * 2:2], mixed[1:amount // 2 * 2:2]
    margin = jnp.minimum(lengths[giver] - 1, bound - lengths[taker]) // 2
    margin = jnp.where((giver == ranking[0]) | (taker == ranking[0]) | (lengths[taker] == 0), 0, jnp.maximum(margin, 0))
    shifted = jax.random.randint(jax.random.fold_in(own, 4), (amount // 2,), 0, 1 << 20) % (margin + 1)
    lengths = lengths.at[giver].add(-shifted).at[taker].add(shifted)
    items = jnp.searchsorted(jnp.cumsum(lengths), jnp.arange(rows * top), side="right").astype(jnp.int32)
    grid = items.reshape(top, rows).T
    grid = grid[jax.random.permutation(jax.random.fold_in(own, 1), rows)]
    turn = jax.random.randint(jax.random.fold_in(own, 2), (rows, 1), 0, top)
    return jnp.take_along_axis(grid, (jnp.arange(top)[None, :] + turn) % top, axis=1)


def shares(count, total, bound, slope, full):
    weights = [(1 << 20) // math.isqrt(grade ** slope) + 1 for grade in range(1, count + 1)]
    largest = bound if full else min(bound, max(-(-total // count), total * weights[0] // sum(weights)))
    least = 1 if total - largest >= count - 1 else 0
    counts, surplus = [largest] + [least] * (count - 1), total - largest - least * (count - 1)
    while surplus > 0:
        candidates = [i for i in range(1, count) if counts[i] < largest] or [i for i in range(1, count) if counts[i] < bound]
        whole, remaining = sum([weights[i] for i in candidates]), surplus
        for i in candidates:
            addition = min(bound - counts[i], max(1, remaining * weights[i] // whole), surplus)
            counts[i] = counts[i] + addition
            surplus = surplus - addition
    return np.array(counts)


def centred(rng, dims, width, limit, split=(), kind=jnp.bfloat16):
    entries = jax.random.normal(rng, dims, jnp.float32) * width
    if len(split) > 0:
        entries = steps_of(rng, dims, split, -0.22, 0.18) * entries
    return jnp.clip(entries, min=-limit, max=limit).astype(kind)


def setup_inputs(seed: int = 0) -> dict:
    key_list = jax.random.split(jax.random.key(seed), 11)
    queries = draw_queries(jax.random.fold_in(key_list[10], 71), 0)
    key_value = draw_key_value(jax.random.fold_in(key_list[10], 71), 0)
    memory = centred(key_list[2], (N_DP * N_EXPERT, MEMLEN, 2, D), 1.0, 6.0, ((0, 512),))
    memory_source = touch_ends(jax.random.randint(key_list[3], (N_DP * N_EXPERT,), 0, 2), jax.random.fold_in(key_list[3], 1), 0, 1).astype(jnp.int32)
    routing_keys = jax.random.split(jax.random.fold_in(key_list[4], 1), TOKENS // TOK_DEV)
    routing_turns = jax.random.permutation(jax.random.fold_in(key_list[4], 3), TOKENS // TOK_DEV)
    routing = jax.vmap(lambda own, number: shared_out(jax.random.fold_in(key_list[4], 2), own, number, TOK_DEV, EXPERTS, TOPK, MOST, 2))(routing_keys, routing_turns).reshape((TOKENS, TOPK))
    router_weight = jnp.clip(0.25 + 0.75 * jax.random.uniform(key_list[5], (TOKENS, TOPK), jnp.float32) ** steps_of(key_list[5], (TOKENS, TOPK), ((0, 512),), -0.2, 0.2), 0.25, 1.0)
    norm_gain = jnp.clip(1.0 + 0.15 * jax.random.normal(key_list[6], (D,), jnp.float32), 0.25, 1.75)
    gate_matrix = centred(key_list[7], (D, EXPERTS * FF), D ** -0.5, 0.125, ((1, 512),))
    up_matrix = centred(key_list[8], (D, EXPERTS * FF), D ** -0.5, 0.125, ((1, 512),))
    down_matrix = centred(key_list[9], (EXPERTS * FF, D), FF ** -0.5, 0.15625, ((0, 512),))
    return {"queries": queries, "key_value": key_value, "memory": memory, "memory_source": memory_source, "routing": routing, "router_weight": router_weight, "norm_gain": norm_gain, "gate_matrix": gate_matrix, "up_matrix": up_matrix, "down_matrix": down_matrix}


def attend(own_queries, own_pairs, recalled):
    token_count = own_queries.shape[0]
    head_size = D // HEADS
    keys_all = jnp.concatenate([recalled[:, 0], own_pairs[:, 0]], axis=0).reshape(-1, HEADS, head_size)
    values_all = jnp.concatenate([recalled[:, 1], own_pairs[:, 1]], axis=0).reshape(-1, HEADS, head_size)
    query_heads = own_queries.reshape(token_count, HEADS, head_size)
    scores = jnp.einsum('thd,khd->htk', query_heads.astype(jnp.float32), keys_all.astype(jnp.float32)) / math.sqrt(head_size)
    memory_rows = recalled.shape[0]
    key_index = jnp.arange(memory_rows + token_count)[None, :]
    query_index = jnp.arange(token_count)[:, None]
    allowed = (key_index < memory_rows) | (key_index - memory_rows <= query_index)
    scores = jnp.where(allowed[None], scores, -1e+30)
    top_score = lax.optimization_barrier(jnp.max(scores, axis=-1, keepdims=True))
    weights = jnp.exp(scores - top_score)
    weights = (weights / lax.optimization_barrier(jnp.sum(weights, axis=-1, keepdims=True))).astype(jnp.bfloat16)
    hidden = jnp.einsum('htk,khd->thd', weights.astype(jnp.float32), values_all.astype(jnp.float32))
    return hidden.reshape(token_count, D).astype(jnp.bfloat16)

def reference(queries, key_value, memory, memory_source, routing, router_weight, norm_gain, gate_matrix, up_matrix, down_matrix):
    device_count = N_DP * N_EXPERT
    device_list = jnp.arange(device_count, dtype=jnp.int32)
    source_device = (device_list // N_EXPERT - 1 - memory_source) % N_DP * N_EXPERT + device_list % N_EXPERT

    def per_device(device):
        first_row = device * TOK_DEV
        own_queries = lax.dynamic_slice_in_dim(queries, first_row, TOK_DEV, 0)
        own_pairs = lax.dynamic_slice_in_dim(key_value, first_row, TOK_DEV, 0)
        recalled = lax.dynamic_index_in_dim(memory, source_device[device], 0, keepdims=False)
        return attend(own_queries, own_pairs, recalled)
    hidden = lax.map(per_device, device_list).reshape(TOKENS, D)
    hidden_wide = hidden.astype(jnp.float32)
    normed = (hidden_wide * lax.rsqrt(lax.optimization_barrier(jnp.mean(hidden_wide * hidden_wide, axis=-1, keepdims=True)) + 1e-06) * norm_gain).astype(jnp.bfloat16)
    extended = jnp.concatenate([normed, jnp.zeros((1, D), jnp.bfloat16)], axis=0)
    chosen_expert = routing[:, 0]
    capacity = N_DP * N_EXPERT * MOST
    slice_units = FF // SLICES

    def per_expert(collected, expert):
        chosen = jnp.nonzero(chosen_expert == expert, size=capacity, fill_value=TOKENS)[0].astype(jnp.int32)
        row_block = extended[chosen]
        gate_block = lax.dynamic_slice_in_dim(gate_matrix, expert * FF, FF, 1)
        up_block = lax.dynamic_slice_in_dim(up_matrix, expert * FF, FF, 1)
        down_block = lax.dynamic_slice_in_dim(down_matrix, expert * FF, FF, 0).reshape(SLICES, slice_units, D)
        gate_part = jnp.dot(row_block, gate_block, preferred_element_type=jnp.float32)
        up_part = jnp.dot(row_block, up_block, preferred_element_type=jnp.float32)
        activation = (jax.nn.silu(gate_part) * up_part).astype(jnp.bfloat16)
        partial_value = jnp.einsum('rsf,sfd->rsd', activation.reshape(capacity, SLICES, slice_units).astype(jnp.float32), down_block.astype(jnp.float32)).astype(jnp.bfloat16)
        combined = lax.optimization_barrier(jnp.sum(partial_value.astype(jnp.float32), axis=1)).astype(jnp.bfloat16)
        return (collected.at[chosen].set(combined), None)
    collected, _ = lax.scan(per_expert, jnp.zeros((TOKENS + 1, D), jnp.bfloat16), jnp.arange(EXPERTS, dtype=jnp.int32))
    expert_out = collected[:TOKENS]
    return (hidden_wide + router_weight * expert_out.astype(jnp.float32)).astype(jnp.bfloat16)
```

```python
import functools
import math

import jax
import jax.numpy as jnp
import numpy as np
from jax import lax
from jax.experimental import pallas as pl
from jax.experimental.pallas import tpu as pltpu
from jax.sharding import Mesh
from jax.sharding import PartitionSpec as P

HEADS = 16
SLICES = 8
MOST = 3
LANES = 128
VMEM_BYTES = 52 * 1024 * 1024

PLACE = ((0, 2, 1, 3), (1, 3, 0, 2), (2, 0, 3, 1), (3, 1, 2, 0))


def spread_pairs():
    return [(PLACE[h][p] * 4 + p, h * 4 + p) for h in range(4) for p in range(4)]


def lift_pairs():
    return [(h * 4 + p, h * 4 + PLACE[h][p]) for h in range(4) for p in range(4)]


def ring(by):
    return [(i, (i + by) % 4) for i in range(4)]


def slots(chosen, rank):
    x = jnp.right_shift(chosen, 4)
    y = jnp.bitwise_and(jnp.right_shift(chosen, 2), 3)
    segment = jnp.bitwise_and(chosen, 3)
    return (y * 16 + segment * 4 + x) * MOST + rank.astype(jnp.int32)


def attend_kernel(
    source,
    queries,
    own_keys,
    own_values,
    near_keys,
    near_values,
    far_keys,
    far_values,
    chosen_column,
    chosen_row,
    gain,
    hidden_out,
    packed_out,
    keys,
    values,
    normed,
    rows,
    sems,
):
    tokens, features = queries.shape

    def fetch(from_keys, from_values):
        first = pltpu.make_async_copy(from_keys, keys, sems.at[0])
        second = pltpu.make_async_copy(from_values, values, sems.at[1])
        first.start()
        second.start()
        first.wait()
        second.wait()

    @pl.when(source[0] == 0)
    def _():
        fetch(near_keys, near_values)

    @pl.when(source[0] != 0)
    def _():
        fetch(far_keys, far_values)

    later = lax.broadcasted_iota(jnp.int32, (tokens, tokens), 1) > lax.broadcasted_iota(
        jnp.int32, (tokens, tokens), 0
    )
    scale = 1.0 / math.sqrt(features // HEADS)
    transposed = (((1,), (1,)), ((), ()))
    squares = jnp.zeros((tokens, LANES), jnp.float32)
    for head in range(HEADS):
        at = slice(head * LANES, (head + 1) * LANES)
        query = queries[:, at]
        far = scale * lax.dot_general(
            query, keys[:, at], transposed, preferred_element_type=jnp.float32
        )
        own = scale * lax.dot_general(
            query, own_keys[:, at], transposed, preferred_element_type=jnp.float32
        )
        own = jnp.where(later, -1e30, own)
        top = jnp.max(jnp.maximum(far, own), axis=1, keepdims=True)
        far = jnp.exp(far - top)
        own = jnp.exp(own - top)
        share = 1.0 / jnp.sum(far + own, axis=1, keepdims=True)
        hidden = jnp.dot(
            (far * share).astype(jnp.bfloat16), values[:, at], preferred_element_type=jnp.float32
        ) + jnp.dot(
            (own * share).astype(jnp.bfloat16),
            own_values[:, at],
            preferred_element_type=jnp.float32,
        )
        hidden = hidden.astype(jnp.bfloat16)
        hidden_out[:, at] = hidden
        wide = hidden.astype(jnp.float32)
        squares += wide * wide
    mean = jnp.sum(squares, axis=1, keepdims=True) / features
    factor = lax.rsqrt(mean + 1e-6)
    for head in range(HEADS):
        at = slice(head * LANES, (head + 1) * LANES)
        normed[:, at] = (hidden_out[:, at].astype(jnp.float32) * factor * gain[:, at]).astype(
            jnp.bfloat16
        )
    same = (chosen_column[...] == chosen_row[...]) & later
    rank = jnp.sum(jnp.where(same, 1.0, 0.0), axis=0, keepdims=True)
    slot = slots(chosen_row[...], rank)
    count = rows.shape[0] // (features // LANES)
    spread = jnp.where(lax.broadcasted_iota(jnp.int32, (count, tokens), 0) == slot, 1.0, 0.0)
    spread = spread.astype(jnp.bfloat16)
    blocks = features // LANES
    packed = jnp.dot(spread, normed[...], preferred_element_type=jnp.float32)
    for block in range(blocks):
        rows[pl.ds(block, count, stride=blocks), :] = packed[:, block * LANES : (block + 1) * LANES]
    packed_out[...] = rows[...].astype(jnp.bfloat16)


def attend(source, queries, own, near, far, chosen, gain):
    tokens, features = queries.shape
    blocks = features // LANES
    count = 64 * MOST
    vmem = pl.BlockSpec(memory_space=pltpu.VMEM)
    anywhere = pl.BlockSpec(memory_space=pl.ANY)
    return pl.pallas_call(
        attend_kernel,
        out_shape=(
            jax.ShapeDtypeStruct((tokens, features), jnp.bfloat16),
            jax.ShapeDtypeStruct((count * blocks, LANES), jnp.bfloat16),
        ),
        in_specs=[pl.BlockSpec(memory_space=pltpu.SMEM)]
        + [vmem] * 3
        + [anywhere] * 4
        + [vmem] * 3,
        out_specs=(vmem, vmem),
        scratch_shapes=[
            pltpu.VMEM((tokens, features), jnp.bfloat16),
            pltpu.VMEM((tokens, features), jnp.bfloat16),
            pltpu.VMEM((tokens, features), jnp.bfloat16),
            pltpu.VMEM((count * blocks, LANES), jnp.float32),
            pltpu.SemaphoreType.DMA((2,)),
        ],
        compiler_params=pltpu.CompilerParams(vmem_limit_bytes=VMEM_BYTES),
        cost_estimate=pl.CostEstimate(
            flops=4 * tokens * 2 * tokens * features,
            bytes_accessed=10 * tokens * features,
            transcendentals=2 * HEADS * tokens * tokens,
        ),
        name="attend",
    )(source, queries, *own, *near, *far, chosen, chosen.reshape(1, tokens), gain)


def experts_kernel(pieces, arrived, *refs):
    total = sum(len(half) for matrix in pieces for half in matrix)
    sources, (out, gate, up, down, rows, tokens, sems) = refs[:total], refs[total:]
    copies, number = [], 0
    for matrix, target in zip(pieces, (gate, up, down)):
        first = 0
        for half in matrix:
            group = []
            for size in half:
                group.append(
                    pltpu.make_async_copy(
                        sources[number], target.at[pl.ds(first, size)], sems.at[number]
                    )
                )
                first += size
                number += 1
            copies.append(group)
    for index in (0, 2, 1, 3, 4, 5):
        for copy in copies[index]:
            copy.start()
    count, features = tokens.shape
    blocks = features // LANES
    rows[...] = arrived[...].astype(jnp.float32)
    for block in range(blocks):
        tokens[:, block * LANES : (block + 1) * LANES] = rows[
            pl.ds(block, count, stride=blocks), :
        ].astype(jnp.bfloat16)
    transposed = (((1,), (1,)), ((), ()))
    middle = gate.shape[0] // 2
    acts = []
    for half in range(2):
        for copy in copies[half] + copies[2 + half]:
            copy.wait()
        at = slice(half * middle, (half + 1) * middle)
        gated = lax.dot_general(
            tokens[...], gate[at, :], transposed, preferred_element_type=jnp.float32
        )
        raised = lax.dot_general(
            tokens[...], up[at, :], transposed, preferred_element_type=jnp.float32
        )
        acts.append((gated / (1.0 + jnp.exp(-gated)) * raised).astype(jnp.bfloat16))
    for copy in copies[4] + copies[5]:
        copy.wait()
    made = jnp.dot(acts[0], down[:middle, :], preferred_element_type=jnp.float32) + jnp.dot(
        acts[1], down[middle:, :], preferred_element_type=jnp.float32
    )
    for block in range(blocks):
        rows[pl.ds(block, count, stride=blocks), :] = made[:, block * LANES : (block + 1) * LANES]
    out[...] = rows[...].astype(jnp.bfloat16)


def experts(arrived, weights):
    features = weights[0][0][0].shape[1]
    count = arrived.shape[0] * arrived.shape[1] // features
    pieces = [[[piece.shape[0] for piece in half] for half in matrix] for matrix in weights]
    units = sum(sum(half) for half in pieces[0])
    flat = [piece for matrix in weights for half in matrix for piece in half]
    vmem = pl.BlockSpec(memory_space=pltpu.VMEM)
    return pl.pallas_call(
        functools.partial(experts_kernel, pieces),
        out_shape=jax.ShapeDtypeStruct(arrived.shape, jnp.bfloat16),
        in_specs=[vmem] + [pl.BlockSpec(memory_space=pl.ANY)] * len(flat),
        out_specs=vmem,
        scratch_shapes=[pltpu.VMEM((units, features), jnp.bfloat16)] * 3
        + [
            pltpu.VMEM(arrived.shape, jnp.float32),
            pltpu.VMEM((count, features), jnp.bfloat16),
            pltpu.SemaphoreType.DMA((len(flat),)),
        ],
        compiler_params=pltpu.CompilerParams(vmem_limit_bytes=VMEM_BYTES),
        cost_estimate=pl.CostEstimate(
            flops=6 * count * features * units,
            bytes_accessed=6 * units * features,
            transcendentals=count * units,
        ),
        name="experts",
    )(arrived, *flat)


def combine_kernel(returned, hidden, chosen_column, chosen_row, weight, out, rows, outputs):
    tokens, features = hidden.shape
    count = outputs.shape[0]
    blocks = features // LANES
    rows[...] = returned[...].astype(jnp.float32)
    for block in range(blocks):
        outputs[:, block * LANES : (block + 1) * LANES] = rows[
            pl.ds(block, count, stride=blocks), :
        ].astype(jnp.bfloat16)
    earlier = lax.broadcasted_iota(jnp.int32, (tokens, tokens), 1) < lax.broadcasted_iota(
        jnp.int32, (tokens, tokens), 0
    )
    same = (chosen_column[...] == chosen_row[...]) & earlier
    rank = jnp.sum(jnp.where(same, 1.0, 0.0), axis=1, keepdims=True)
    slot = slots(chosen_column[...], rank)
    pick = jnp.where(lax.broadcasted_iota(jnp.int32, (tokens, count), 1) == slot, 1.0, 0.0)
    picked = jnp.dot(pick.astype(jnp.bfloat16), outputs[...], preferred_element_type=jnp.float32)
    out[...] = (hidden[...].astype(jnp.float32) + weight[...] * picked).astype(jnp.bfloat16)


def combine(returned, hidden, chosen, weight):
    tokens, features = hidden.shape
    count = 64 * MOST
    vmem = pl.BlockSpec(memory_space=pltpu.VMEM)
    return pl.pallas_call(
        combine_kernel,
        out_shape=jax.ShapeDtypeStruct(hidden.shape, jnp.bfloat16),
        in_specs=[vmem] * 5,
        out_specs=vmem,
        scratch_shapes=[
            pltpu.VMEM(returned.shape, jnp.float32),
            pltpu.VMEM((count, features), jnp.bfloat16),
        ],
        compiler_params=pltpu.CompilerParams(vmem_limit_bytes=VMEM_BYTES),
        name="combine",
    )(returned, hidden, chosen, chosen.reshape(1, tokens), weight)


def gathered(matrix, which):
    moved = lax.ppermute(matrix, ("x", "p"), spread_pairs())
    own = lax.ppermute(moved, ("x", "p"), lift_pairs())
    left = lax.ppermute(own, "x", ring(1))
    right = lax.ppermute(own, "x", ring(-1))
    if which == 0:
        far = [lax.ppermute(left, "x", ring(1))]
    elif which == 1:
        far = [lax.ppermute(right, "x", ring(-1))]
    else:
        cut = 96
        far = [lax.ppermute(left[:cut], "x", ring(1)), lax.ppermute(right[cut:], "x", ring(-1))]
    other = lambda piece: lax.ppermute(piece, "c", [(0, 1), (1, 0)])
    first, second = [own, left], [right, *far]
    return [first + [other(piece) for piece in first], second + [other(piece) for piece in second]]


def passed_along(block, by):
    return lax.ppermute(block, ("x", "y"), [(i, (i + by) % 16) for i in range(16)])


def per_device(
    queries,
    key_value,
    memory,
    memory_source,
    routing,
    router_weight,
    norm_gain,
    gate_matrix,
    up_matrix,
    down_matrix,
):
    features = queries.shape[1]
    kept = [memory[0, :, 0], memory[0, :, 1]]
    near = [passed_along(block, 1) for block in kept]
    far = [passed_along(block, 2) for block in kept]
    weights = [
        gathered(matrix, which)
        for which, matrix in enumerate((gate_matrix.T, up_matrix.T, down_matrix))
    ]
    own = [key_value[:, 0], key_value[:, 1]]
    hidden, packed = attend(
        memory_source, queries, own, near, far, routing, norm_gain.reshape(1, features)
    )
    chunks = packed.reshape(64, -1, LANES)
    arrived = lax.all_to_all(chunks, ("y", "s", "p"), 0, 0, tiled=True)
    made = experts(arrived.reshape(packed.shape), weights)
    returned = lax.all_to_all(made.reshape(chunks.shape), ("y", "s", "p"), 0, 0, tiled=True)
    return combine(returned.reshape(packed.shape), hidden, routing, router_weight)


def solution(mesh):
    every = ("x", "y", "s", "p", "c")
    fine = Mesh(np.asarray(mesh.devices).reshape(4, 4, 4, 4, 2), every)
    return jax.shard_map(
        per_device,
        mesh=fine,
        in_specs=(
            P(every, None),
            P(every, None, None),
            P(every, None, None, None),
            P(every),
            P(every, None),
            P(every, None),
            P(),
            P(None, every),
            P(None, every),
            P(every, None),
        ),
        out_specs=P(every, None),
        check_vma=False,
    )
```

```python
import math

import jax
import jax.numpy as jnp
import numpy as np
from jax import lax
from jax.experimental import pallas as pl
from jax.experimental.pallas import tpu as pltpu
from jax.sharding import Mesh
from jax.sharding import PartitionSpec as P

HEADS = 16
MOST = 3
LANES = 128
VMEM_BYTES = 32 * 1024 * 1024

PLACE = ((0, 2, 1, 3), (1, 3, 0, 2), (2, 0, 3, 1), (3, 1, 2, 0))


def spread_pairs():
    return [(PLACE[h][p] * 4 + p, h * 4 + p) for h in range(4) for p in range(4)]


def lift_pairs():
    return [(h * 4 + p, h * 4 + PLACE[h][p]) for h in range(4) for p in range(4)]


def ring(by):
    return [(i, (i + by) % 4) for i in range(4)]


def slots(chosen, rank):
    x = jnp.right_shift(chosen, 4)
    y = jnp.bitwise_and(jnp.right_shift(chosen, 2), 3)
    segment = jnp.bitwise_and(chosen, 3)
    return (y * 16 + segment * 4 + x) * MOST + rank.astype(jnp.int32)


def attend_kernel(
    source,
    queries,
    own,
    near,
    far_off,
    chosen_column,
    chosen_row,
    gain,
    hidden_out,
    packed_out,
    recalled,
    normed,
    rows,
    sem,
):
    tokens, features = queries.shape

    def fetch(block):
        copy = pltpu.make_async_copy(block, recalled, sem)
        copy.start()
        copy.wait()

    @pl.when(source[0] == 0)
    def _():
        fetch(near)

    @pl.when(source[0] != 0)
    def _():
        fetch(far_off)

    later = lax.broadcasted_iota(jnp.int32, (tokens, tokens), 1) > lax.broadcasted_iota(
        jnp.int32, (tokens, tokens), 0
    )
    scale = 1.0 / math.sqrt(features // HEADS)
    transposed = (((1,), (1,)), ((), ()))
    squares = jnp.zeros((tokens, LANES), jnp.float32)
    for head in range(HEADS):
        at = slice(head * LANES, (head + 1) * LANES)
        query = queries[:, at]
        far = scale * lax.dot_general(
            query, recalled[0, :, at], transposed, preferred_element_type=jnp.float32
        )
        here = scale * lax.dot_general(
            query, own[0, :, at], transposed, preferred_element_type=jnp.float32
        )
        here = jnp.where(later, -1e30, here)
        top = jnp.max(jnp.maximum(far, here), axis=1, keepdims=True)
        far = jnp.exp(far - top)
        here = jnp.exp(here - top)
        share = 1.0 / jnp.sum(far + here, axis=1, keepdims=True)
        hidden = jnp.dot(
            (far * share).astype(jnp.bfloat16),
            recalled[1, :, at],
            preferred_element_type=jnp.float32,
        ) + jnp.dot(
            (here * share).astype(jnp.bfloat16), own[1, :, at], preferred_element_type=jnp.float32
        )
        hidden = hidden.astype(jnp.bfloat16)
        hidden_out[:, at] = hidden
        wide = hidden.astype(jnp.float32)
        squares += wide * wide
    mean = jnp.sum(squares, axis=1, keepdims=True) / features
    factor = lax.rsqrt(mean + 1e-6)
    for head in range(HEADS):
        at = slice(head * LANES, (head + 1) * LANES)
        normed[:, at] = (hidden_out[:, at].astype(jnp.float32) * factor * gain[:, at]).astype(
            jnp.bfloat16
        )
    same = (chosen_column[...] == chosen_row[...]) & later
    rank = jnp.sum(jnp.where(same, 1.0, 0.0), axis=0, keepdims=True)
    slot = slots(chosen_row[...], rank)
    count = rows.shape[0] // (features // LANES)
    spread = jnp.where(lax.broadcasted_iota(jnp.int32, (count, tokens), 0) == slot, 1.0, 0.0)
    spread = spread.astype(jnp.bfloat16)
    blocks = features // LANES
    packed = jnp.dot(spread, normed[...], preferred_element_type=jnp.float32)
    for block in range(blocks):
        rows[pl.ds(block, count, stride=blocks), :] = packed[:, block * LANES : (block + 1) * LANES]
    packed_out[...] = rows[...].astype(jnp.bfloat16)


def attend(source, queries, own, near, far, chosen, gain):
    tokens, features = queries.shape
    blocks = features // LANES
    count = 64 * MOST
    vmem = pl.BlockSpec(memory_space=pltpu.VMEM)
    anywhere = pl.BlockSpec(memory_space=pl.ANY)
    return pl.pallas_call(
        attend_kernel,
        out_shape=(
            jax.ShapeDtypeStruct((tokens, features), jnp.bfloat16),
            jax.ShapeDtypeStruct((count * blocks, LANES), jnp.bfloat16),
        ),
        in_specs=[pl.BlockSpec(memory_space=pltpu.SMEM)]
        + [vmem] * 2
        + [anywhere] * 2
        + [vmem] * 3,
        out_specs=(vmem, vmem),
        scratch_shapes=[
            pltpu.VMEM((2, tokens, features), jnp.bfloat16),
            pltpu.VMEM((tokens, features), jnp.bfloat16),
            pltpu.VMEM((count * blocks, LANES), jnp.float32),
            pltpu.SemaphoreType.DMA,
        ],
        compiler_params=pltpu.CompilerParams(vmem_limit_bytes=VMEM_BYTES),
        cost_estimate=pl.CostEstimate(
            flops=4 * tokens * 2 * tokens * features,
            bytes_accessed=10 * tokens * features,
            transcendentals=2 * HEADS * tokens * tokens,
        ),
        name="attend",
    )(source, queries, own, near, far, chosen, chosen.reshape(1, tokens), gain)


def experts_kernel(arrived, *refs):
    gates, ups, downs, (out, rows, tokens) = refs[:4], refs[4:8], refs[8:13], refs[13:]
    count, features = tokens.shape
    blocks = features // LANES
    rows[...] = arrived[...].astype(jnp.float32)
    for block in range(blocks):
        tokens[:, block * LANES : (block + 1) * LANES] = rows[
            pl.ds(block, count, stride=blocks), :
        ].astype(jnp.bfloat16)
    transposed = (((1,), (1,)), ((), ()))
    acts = []
    for gate, up in zip(gates, ups):
        gated = lax.dot_general(
            tokens[...], gate[...], transposed, preferred_element_type=jnp.float32
        )
        raised = lax.dot_general(
            tokens[...], up[...], transposed, preferred_element_type=jnp.float32
        )
        acts.append((gated / (1.0 + jnp.exp(-gated)) * raised).astype(jnp.bfloat16))
    middle = features // 2
    for half in range(2):
        at = slice(half * middle, (half + 1) * middle)
        made = jnp.dot(acts[3], downs[3 + half][...], preferred_element_type=jnp.float32)
        for act, down in zip(acts[:3], downs[:3]):
            made += jnp.dot(act, down[:, at], preferred_element_type=jnp.float32)
        for block in range(blocks // 2):
            rows[pl.ds(half * (blocks // 2) + block, count, stride=blocks), :] = made[
                :, block * LANES : (block + 1) * LANES
            ]
    out[...] = rows[...].astype(jnp.bfloat16)


def experts(arrived, weights, name):
    gates, ups, downs = weights
    units, features = gates[0].shape
    count = arrived.shape[0] * arrived.shape[1] // features
    vmem = pl.BlockSpec(memory_space=pltpu.VMEM)
    return pl.pallas_call(
        experts_kernel,
        out_shape=jax.ShapeDtypeStruct(arrived.shape, jnp.bfloat16),
        in_specs=[vmem] * (1 + len(gates) + len(ups) + len(downs)),
        out_specs=vmem,
        scratch_shapes=[
            pltpu.VMEM(arrived.shape, jnp.float32),
            pltpu.VMEM((count, features), jnp.bfloat16),
        ],
        compiler_params=pltpu.CompilerParams(vmem_limit_bytes=VMEM_BYTES),
        cost_estimate=pl.CostEstimate(
            flops=6 * count * features * units * 4,
            bytes_accessed=6 * units * 4 * features,
            transcendentals=count * units * 4,
        ),
        name=name,
    )(arrived, *gates, *ups, *downs)


def combine_kernel(returned, hidden, chosen_column, chosen_row, weight, out, rows, outputs):
    tokens, features = hidden.shape
    count = outputs.shape[0]
    blocks = features // LANES
    rows[...] = returned[...].astype(jnp.float32)
    for block in range(blocks):
        outputs[:, block * LANES : (block + 1) * LANES] = rows[
            pl.ds(block, count, stride=blocks), :
        ].astype(jnp.bfloat16)
    earlier = lax.broadcasted_iota(jnp.int32, (tokens, tokens), 1) < lax.broadcasted_iota(
        jnp.int32, (tokens, tokens), 0
    )
    same = (chosen_column[...] == chosen_row[...]) & earlier
    rank = jnp.sum(jnp.where(same, 1.0, 0.0), axis=1, keepdims=True)
    slot = slots(chosen_column[...], rank)
    pick = jnp.where(lax.broadcasted_iota(jnp.int32, (tokens, count), 1) == slot, 1.0, 0.0)
    picked = jnp.dot(pick.astype(jnp.bfloat16), outputs[...], preferred_element_type=jnp.float32)
    out[...] = (hidden[...].astype(jnp.float32) + weight[...] * picked).astype(jnp.bfloat16)


def combine(returned, hidden, chosen, weight):
    tokens, features = hidden.shape
    count = 64 * MOST
    vmem = pl.BlockSpec(memory_space=pltpu.VMEM)
    return pl.pallas_call(
        combine_kernel,
        out_shape=jax.ShapeDtypeStruct(hidden.shape, jnp.bfloat16),
        in_specs=[vmem] * 5,
        out_specs=vmem,
        scratch_shapes=[
            pltpu.VMEM(returned.shape, jnp.float32),
            pltpu.VMEM((count, features), jnp.bfloat16),
        ],
        compiler_params=pltpu.CompilerParams(vmem_limit_bytes=VMEM_BYTES),
        name="combine",
    )(returned, hidden, chosen, chosen.reshape(1, tokens), weight)


def after(value, *others):
    return lax.optimization_barrier((value, *others))[0]


def swapped(rows):
    return lax.ppermute(rows, "c", [(0, 1), (1, 0)])


def passed_along(block, by):
    return lax.ppermute(block, ("x", "y"), [(i, (i + by) % 16) for i in range(16)])


def per_device(
    queries,
    key_value,
    memory,
    memory_source,
    routing,
    router_weight,
    norm_gain,
    gate_matrix,
    up_matrix,
    down_matrix,
):
    features = queries.shape[1]
    kept = memory[0].transpose(1, 0, 2)
    near = passed_along(kept, 1)
    far = passed_along(kept, 2)
    moved = [
        lax.ppermute(matrix, ("x", "p"), spread_pairs())
        for matrix in (gate_matrix.T, up_matrix.T, down_matrix)
    ]
    placed = [lax.ppermute(matrix, ("x", "p"), lift_pairs()) for matrix in moved]
    left = [lax.ppermute(matrix, "x", ring(1)) for matrix in placed]
    right = [lax.ppermute(matrix, "x", ring(-1)) for matrix in placed]
    middle = features // 2
    across = [
        [lax.ppermute(left[0], "x", ring(1))],
        [lax.ppermute(right[1], "x", ring(-1))],
        [
            lax.ppermute(left[2][:, :middle], "x", ring(1)),
            lax.ppermute(right[2][:, middle:], "x", ring(-1)),
        ],
    ]
    weights = [
        [own, before, behind, *beyond]
        for own, before, behind, beyond in zip(placed, left, right, across)
    ]
    hidden, packed = attend(
        memory_source,
        after(queries, placed[0], placed[1], moved[2]),
        key_value.transpose(1, 0, 2),
        near,
        far,
        routing,
        norm_gain.reshape(1, features),
    )
    packed = after(packed, left[0], right[0], placed[2], left[1], right[1])
    chunks = packed.reshape(64, -1, LANES)
    arrived = lax.all_to_all(chunks, ("y", "s", "p"), 0, 0, tiled=True).reshape(packed.shape)
    partner = swapped(after(arrived, across[0], across[1], across[2]))
    lent = swapped(experts(partner, weights, "partner_experts"))
    made = experts(arrived, weights, "own_experts")
    made = (made.astype(jnp.float32) + lent.astype(jnp.float32)).astype(jnp.bfloat16)
    returned = lax.all_to_all(made.reshape(chunks.shape), ("y", "s", "p"), 0, 0, tiled=True)
    return combine(returned.reshape(packed.shape), hidden, routing, router_weight)


def solution(mesh):
    every = ("x", "y", "s", "p", "c")
    fine = Mesh(np.asarray(mesh.devices).reshape(4, 4, 4, 4, 2), every)
    return jax.shard_map(
        per_device,
        mesh=fine,
        in_specs=(
            P(every, None),
            P(every, None, None),
            P(every, None, None, None),
            P(every),
            P(every, None),
            P(every, None),
            P(),
            P(None, every),
            P(None, every),
            P(every, None),
        ),
        out_specs=P(every, None),
        check_vma=False,
    )
```

```python
import math

import jax
import jax.numpy as jnp
import numpy as np
from jax import lax
from jax.experimental import pallas as pl
from jax.experimental.pallas import tpu as pltpu
from jax.sharding import Mesh
from jax.sharding import PartitionSpec as P

HEADS = 16
MOST = 3
LANES = 128
VMEM_BYTES = 14 * 1024 * 1024

PLACE = ((0, 2, 1, 3), (1, 3, 0, 2), (2, 0, 3, 1), (3, 1, 2, 0))


def spread_pairs():
    return [(PLACE[h][p] * 4 + p, h * 4 + p) for h in range(4) for p in range(4)]


def lift_pairs():
    return [(h * 4 + p, h * 4 + PLACE[h][p]) for h in range(4) for p in range(4)]


def ring(by):
    return [(i, (i + by) % 4) for i in range(4)]


def slots(chosen, rank):
    x = jnp.right_shift(chosen, 4)
    y = jnp.bitwise_and(jnp.right_shift(chosen, 2), 3)
    segment = jnp.bitwise_and(chosen, 3)
    return (y * 16 + segment * 4 + x) * MOST + rank.astype(jnp.int32)


def attend_kernel(
    source,
    queries,
    own,
    near,
    far_off,
    chosen_column,
    chosen_row,
    gain,
    hidden_out,
    packed_out,
    recalled,
    normed,
    rows,
    sem,
):
    tokens, features = queries.shape

    def fetch(block):
        copy = pltpu.make_async_copy(block, recalled, sem)
        copy.start()
        copy.wait()

    @pl.when(source[0] == 0)
    def _():
        fetch(near)

    @pl.when(source[0] != 0)
    def _():
        fetch(far_off)

    later = lax.broadcasted_iota(jnp.int32, (tokens, tokens), 1) > lax.broadcasted_iota(
        jnp.int32, (tokens, tokens), 0
    )
    scale = 1.0 / math.sqrt(features // HEADS)
    transposed = (((1,), (1,)), ((), ()))
    squares = jnp.zeros((tokens, LANES), jnp.float32)
    for head in range(HEADS):
        at = slice(head * LANES, (head + 1) * LANES)
        query = queries[:, at]
        far = scale * lax.dot_general(
            query, recalled[0, :, at], transposed, preferred_element_type=jnp.float32
        )
        here = scale * lax.dot_general(
            query, own[0, :, at], transposed, preferred_element_type=jnp.float32
        )
        here = jnp.where(later, -1e30, here)
        top = jnp.max(jnp.maximum(far, here), axis=1, keepdims=True)
        far = jnp.exp(far - top)
        here = jnp.exp(here - top)
        share = 1.0 / jnp.sum(far + here, axis=1, keepdims=True)
        hidden = jnp.dot(
            (far * share).astype(jnp.bfloat16),
            recalled[1, :, at],
            preferred_element_type=jnp.float32,
        ) + jnp.dot(
            (here * share).astype(jnp.bfloat16), own[1, :, at], preferred_element_type=jnp.float32
        )
        hidden = hidden.astype(jnp.bfloat16)
        hidden_out[:, at] = hidden
        wide = hidden.astype(jnp.float32)
        squares += wide * wide
    mean = jnp.sum(squares, axis=1, keepdims=True) / features
    factor = lax.rsqrt(mean + 1e-6)
    for head in range(HEADS):
        at = slice(head * LANES, (head + 1) * LANES)
        normed[:, at] = (hidden_out[:, at].astype(jnp.float32) * factor * gain[:, at]).astype(
            jnp.bfloat16
        )
    same = (chosen_column[...] == chosen_row[...]) & later
    rank = jnp.sum(jnp.where(same, 1.0, 0.0), axis=0, keepdims=True)
    slot = slots(chosen_row[...], rank)
    count = rows.shape[0] // (features // LANES)
    spread = jnp.where(lax.broadcasted_iota(jnp.int32, (count, tokens), 0) == slot, 1.0, 0.0)
    spread = spread.astype(jnp.bfloat16)
    blocks = features // LANES
    packed = jnp.dot(spread, normed[...], preferred_element_type=jnp.float32)
    for block in range(blocks):
        rows[pl.ds(block, count, stride=blocks), :] = packed[:, block * LANES : (block + 1) * LANES]
    packed_out[...] = rows[...].astype(jnp.bfloat16)


def attend(source, queries, own, near, far, chosen, gain):
    tokens, features = queries.shape
    blocks = features // LANES
    count = 64 * MOST
    vmem = pl.BlockSpec(memory_space=pltpu.VMEM)
    anywhere = pl.BlockSpec(memory_space=pl.ANY)
    return pl.pallas_call(
        attend_kernel,
        out_shape=(
            jax.ShapeDtypeStruct((tokens, features), jnp.bfloat16),
            jax.ShapeDtypeStruct((count * blocks, LANES), jnp.bfloat16),
        ),
        in_specs=[pl.BlockSpec(memory_space=pltpu.SMEM)]
        + [vmem] * 2
        + [anywhere] * 2
        + [vmem] * 3,
        out_specs=(vmem, vmem),
        scratch_shapes=[
            pltpu.VMEM((2, tokens, features), jnp.bfloat16),
            pltpu.VMEM((tokens, features), jnp.bfloat16),
            pltpu.VMEM((count * blocks, LANES), jnp.float32),
            pltpu.SemaphoreType.DMA,
        ],
        compiler_params=pltpu.CompilerParams(vmem_limit_bytes=VMEM_BYTES),
        cost_estimate=pl.CostEstimate(
            flops=4 * tokens * 2 * tokens * features,
            bytes_accessed=10 * tokens * features,
            transcendentals=2 * HEADS * tokens * tokens,
        ),
        name="attend",
    )(source, queries, own, near, far, chosen, chosen.reshape(1, tokens), gain)


def experts_kernel(arrived, *refs):
    gates, ups, downs, (out, rows, tokens) = refs[:4], refs[4:8], refs[8:12], refs[12:]
    count, features = tokens.shape
    blocks = features // LANES
    rows[...] = arrived[...].astype(jnp.float32)
    for block in range(blocks):
        tokens[:, block * LANES : (block + 1) * LANES] = rows[
            pl.ds(block, count, stride=blocks), :
        ].astype(jnp.bfloat16)
    transposed = (((1,), (1,)), ((), ()))
    acts = []
    for gate, up in zip(gates, ups):
        gated = lax.dot_general(
            tokens[...], gate[...], transposed, preferred_element_type=jnp.float32
        )
        raised = lax.dot_general(
            tokens[...], up[...], transposed, preferred_element_type=jnp.float32
        )
        acts.append((gated / (1.0 + jnp.exp(-gated)) * raised).astype(jnp.bfloat16))
    made = jnp.zeros((count, features), jnp.float32)
    for act, down in zip(acts, downs):
        made += jnp.dot(act, down[...], preferred_element_type=jnp.float32)
    for block in range(blocks):
        rows[pl.ds(block, count, stride=blocks), :] = made[:, block * LANES : (block + 1) * LANES]
    out[...] = rows[...].astype(jnp.bfloat16)


def experts(arrived, weights, name):
    gates, ups, downs = weights
    units, features = gates[0].shape
    count = arrived.shape[0] * arrived.shape[1] // features
    vmem = pl.BlockSpec(memory_space=pltpu.VMEM)
    return pl.pallas_call(
        experts_kernel,
        out_shape=jax.ShapeDtypeStruct(arrived.shape, jnp.bfloat16),
        in_specs=[vmem] * (1 + len(gates) + len(ups) + len(downs)),
        out_specs=vmem,
        scratch_shapes=[
            pltpu.VMEM(arrived.shape, jnp.float32),
            pltpu.VMEM((count, features), jnp.bfloat16),
        ],
        compiler_params=pltpu.CompilerParams(vmem_limit_bytes=VMEM_BYTES),
        cost_estimate=pl.CostEstimate(
            flops=6 * count * features * units * 4,
            bytes_accessed=6 * units * 4 * features,
            transcendentals=count * units * 4,
        ),
        name=name,
    )(arrived, *gates, *ups, *downs)


def combine_kernel(returned, hidden, chosen_column, chosen_row, weight, out, rows, outputs):
    tokens, features = hidden.shape
    count = outputs.shape[0]
    blocks = features // LANES
    rows[...] = returned[...].astype(jnp.float32)
    for block in range(blocks):
        outputs[:, block * LANES : (block + 1) * LANES] = rows[
            pl.ds(block, count, stride=blocks), :
        ].astype(jnp.bfloat16)
    earlier = lax.broadcasted_iota(jnp.int32, (tokens, tokens), 1) < lax.broadcasted_iota(
        jnp.int32, (tokens, tokens), 0
    )
    same = (chosen_column[...] == chosen_row[...]) & earlier
    rank = jnp.sum(jnp.where(same, 1.0, 0.0), axis=1, keepdims=True)
    slot = slots(chosen_column[...], rank)
    pick = jnp.where(lax.broadcasted_iota(jnp.int32, (tokens, count), 1) == slot, 1.0, 0.0)
    picked = jnp.dot(pick.astype(jnp.bfloat16), outputs[...], preferred_element_type=jnp.float32)
    out[...] = (hidden[...].astype(jnp.float32) + weight[...] * picked).astype(jnp.bfloat16)


def combine(returned, hidden, chosen, weight):
    tokens, features = hidden.shape
    count = 64 * MOST
    vmem = pl.BlockSpec(memory_space=pltpu.VMEM)
    return pl.pallas_call(
        combine_kernel,
        out_shape=jax.ShapeDtypeStruct(hidden.shape, jnp.bfloat16),
        in_specs=[vmem] * 5,
        out_specs=vmem,
        scratch_shapes=[
            pltpu.VMEM(returned.shape, jnp.float32),
            pltpu.VMEM((count, features), jnp.bfloat16),
        ],
        compiler_params=pltpu.CompilerParams(vmem_limit_bytes=VMEM_BYTES),
        name="combine",
    )(returned, hidden, chosen, chosen.reshape(1, tokens), weight)


def after(value, *others):
    return lax.optimization_barrier((value, *others))[0]


def swapped(rows):
    return lax.ppermute(rows, "c", [(0, 1), (1, 0)])


def passed_along(block):
    return lax.ppermute(block, ("x", "y"), [(i, (i + 1) % 16) for i in range(16)])


def per_device(
    queries,
    key_value,
    memory,
    memory_source,
    routing,
    router_weight,
    norm_gain,
    gate_matrix,
    up_matrix,
    down_matrix,
):
    features = queries.shape[1]
    kept = memory[0].transpose(1, 0, 2)
    near = passed_along(kept)
    far = passed_along(near)
    moved = [
        lax.ppermute(matrix, ("x", "p"), spread_pairs())
        for matrix in (gate_matrix.T, up_matrix.T, down_matrix)
    ]
    placed = [lax.ppermute(matrix, ("x", "p"), lift_pairs()) for matrix in moved]
    left = [lax.ppermute(matrix, "x", ring(1)) for matrix in placed]
    right = [lax.ppermute(matrix, "x", ring(-1)) for matrix in placed]
    across = [lax.ppermute(matrix, "x", ring(-1)) for matrix in right]
    weights = [
        [own, before, behind, beyond]
        for own, before, behind, beyond in zip(placed, left, right, across)
    ]
    hidden, packed = attend(
        memory_source,
        after(queries, placed[0], placed[1], moved[2]),
        key_value.transpose(1, 0, 2),
        near,
        far,
        routing,
        norm_gain.reshape(1, features),
    )
    packed = after(packed, *left, *right)
    chunks = packed.reshape(64, -1, LANES)
    arrived = lax.all_to_all(chunks, ("y", "s", "p"), 0, 0, tiled=True).reshape(packed.shape)
    partner = swapped(after(arrived, *across))
    lent = swapped(experts(partner, weights, "partner_experts"))
    made = experts(arrived, weights, "own_experts")
    made = (made.astype(jnp.float32) + lent.astype(jnp.float32)).astype(jnp.bfloat16)
    returned = lax.all_to_all(made.reshape(chunks.shape), ("y", "s", "p"), 0, 0, tiled=True)
    return combine(returned.reshape(packed.shape), hidden, routing, router_weight)


def solution(mesh):
    every = ("x", "y", "s", "p", "c")
    fine = Mesh(np.asarray(mesh.devices).reshape(4, 4, 4, 4, 2), every)
    return jax.shard_map(
        per_device,
        mesh=fine,
        in_specs=(
            P(every, None),
            P(every, None, None),
            P(every, None, None, None),
            P(every),
            P(every, None),
            P(every, None),
            P(),
            P(None, every),
            P(None, every),
            P(every, None),
        ),
        out_specs=P(every, None),
        check_vma=False,
    )
```

```python
import functools
import math

import jax
import jax.numpy as jnp
import numpy as np
from jax import lax
from jax.experimental import pallas as pl
from jax.experimental.pallas import tpu as pltpu
from jax.sharding import Mesh
from jax.sharding import PartitionSpec as P

HEADS = 16
MOST = 3
LANES = 128
VMEM_BYTES = 16 * 1024 * 1024

PLACE = ((0, 2, 1, 3), (1, 3, 0, 2), (2, 0, 3, 1), (3, 1, 2, 0))


def spread_pairs():
    return [(PLACE[h][p] * 4 + p, h * 4 + p) for h in range(4) for p in range(4)]


def lift_pairs():
    return [(h * 4 + p, h * 4 + PLACE[h][p]) for h in range(4) for p in range(4)]


def ring(by):
    return [(i, (i + by) % 4) for i in range(4)]


def slots(chosen, rank):
    x = jnp.right_shift(chosen, 4)
    y = jnp.bitwise_and(jnp.right_shift(chosen, 2), 3)
    segment = jnp.bitwise_and(chosen, 3)
    return (y * 16 + segment * 4 + x) * MOST + rank.astype(jnp.int32)


def attend_kernel(
    source,
    queries,
    own,
    near,
    far_off,
    chosen_column,
    chosen_row,
    gain,
    hidden_out,
    packed_out,
    recalled,
    normed,
    rows,
    sem,
):
    tokens, features = queries.shape

    def fetch(block):
        copy = pltpu.make_async_copy(block, recalled, sem)
        copy.start()
        copy.wait()

    @pl.when(source[0] == 0)
    def _():
        fetch(near)

    @pl.when(source[0] != 0)
    def _():
        fetch(far_off)

    later = lax.broadcasted_iota(jnp.int32, (tokens, tokens), 1) > lax.broadcasted_iota(
        jnp.int32, (tokens, tokens), 0
    )
    scale = 1.0 / math.sqrt(features // HEADS)
    transposed = (((1,), (1,)), ((), ()))
    squares = jnp.zeros((tokens, LANES), jnp.float32)
    for head in range(HEADS):
        at = slice(head * LANES, (head + 1) * LANES)
        query = queries[:, at]
        far = scale * lax.dot_general(
            query, recalled[0, :, at], transposed, preferred_element_type=jnp.float32
        )
        here = scale * lax.dot_general(
            query, own[0, :, at], transposed, preferred_element_type=jnp.float32
        )
        here = jnp.where(later, -1e30, here)
        top = jnp.max(jnp.maximum(far, here), axis=1, keepdims=True)
        far = jnp.exp(far - top)
        here = jnp.exp(here - top)
        share = 1.0 / jnp.sum(far + here, axis=1, keepdims=True)
        hidden = jnp.dot(
            (far * share).astype(jnp.bfloat16),
            recalled[1, :, at],
            preferred_element_type=jnp.float32,
        ) + jnp.dot(
            (here * share).astype(jnp.bfloat16), own[1, :, at], preferred_element_type=jnp.float32
        )
        hidden = hidden.astype(jnp.bfloat16)
        hidden_out[:, at] = hidden
        wide = hidden.astype(jnp.float32)
        squares += wide * wide
    mean = jnp.sum(squares, axis=1, keepdims=True) / features
    factor = lax.rsqrt(mean + 1e-6)
    for head in range(HEADS):
        at = slice(head * LANES, (head + 1) * LANES)
        normed[:, at] = (hidden_out[:, at].astype(jnp.float32) * factor * gain[:, at]).astype(
            jnp.bfloat16
        )
    same = (chosen_column[...] == chosen_row[...]) & later
    rank = jnp.sum(jnp.where(same, 1.0, 0.0), axis=0, keepdims=True)
    slot = slots(chosen_row[...], rank)
    count = rows.shape[0] // (features // LANES)
    spread = jnp.where(lax.broadcasted_iota(jnp.int32, (count, tokens), 0) == slot, 1.0, 0.0)
    spread = spread.astype(jnp.bfloat16)
    blocks = features // LANES
    packed = jnp.dot(spread, normed[...], preferred_element_type=jnp.float32)
    for block in range(blocks):
        rows[pl.ds(block, count, stride=blocks), :] = packed[:, block * LANES : (block + 1) * LANES]
    packed_out[...] = rows[...].astype(jnp.bfloat16)


def attend(source, queries, own, near, far, chosen, gain):
    tokens, features = queries.shape
    blocks = features // LANES
    count = 64 * MOST
    vmem = pl.BlockSpec(memory_space=pltpu.VMEM)
    anywhere = pl.BlockSpec(memory_space=pl.ANY)
    return pl.pallas_call(
        attend_kernel,
        out_shape=(
            jax.ShapeDtypeStruct((tokens, features), jnp.bfloat16),
            jax.ShapeDtypeStruct((count * blocks, LANES), jnp.bfloat16),
        ),
        in_specs=[pl.BlockSpec(memory_space=pltpu.SMEM)]
        + [vmem] * 2
        + [anywhere] * 2
        + [vmem] * 3,
        out_specs=(vmem, vmem),
        scratch_shapes=[
            pltpu.VMEM((2, tokens, features), jnp.bfloat16),
            pltpu.VMEM((tokens, features), jnp.bfloat16),
            pltpu.VMEM((count * blocks, LANES), jnp.float32),
            pltpu.SemaphoreType.DMA,
        ],
        compiler_params=pltpu.CompilerParams(vmem_limit_bytes=VMEM_BYTES),
        cost_estimate=pl.CostEstimate(
            flops=4 * tokens * 2 * tokens * features,
            bytes_accessed=10 * tokens * features,
            transcendentals=2 * HEADS * tokens * tokens,
        ),
        name="attend",
    )(source, queries, own, near, far, chosen, chosen.reshape(1, tokens), gain)


def experts_kernel(pieces, arrived, partner, *refs):
    sources = refs[: len(pieces)]
    out, lent, gate, up, down, rows, tokens, sems = refs[len(pieces) :]
    copies = ([], [], [])
    for number, (source, (matrix, row, column)) in enumerate(zip(sources, pieces)):
        units, width = source.shape
        target = (gate, up, down)[matrix].at[pl.ds(row, units), pl.ds(column, width)]
        copy = pltpu.make_async_copy(source, target, sems.at[number])
        copy.start()
        copies[matrix].append(copy)
    count, features = tokens.shape[0] // 2, tokens.shape[1]
    blocks = features // LANES
    for half, block_rows in enumerate((arrived, partner)):
        rows[half] = block_rows[...].astype(jnp.float32)
        for block in range(blocks):
            tokens[half * count : (half + 1) * count, block * LANES : (block + 1) * LANES] = rows[
                half, pl.ds(block, count, stride=blocks), :
            ].astype(jnp.bfloat16)
    for copy in copies[0] + copies[1]:
        copy.wait()
    transposed = (((1,), (1,)), ((), ()))
    gated = lax.dot_general(
        tokens[...], gate[...], transposed, preferred_element_type=jnp.float32
    )
    raised = lax.dot_general(tokens[...], up[...], transposed, preferred_element_type=jnp.float32)
    act = (gated / (1.0 + jnp.exp(-gated)) * raised).astype(jnp.bfloat16)
    for copy in copies[2]:
        copy.wait()
    for half, target in ((1, lent), (0, out)):
        made = jnp.dot(
            act[half * count : (half + 1) * count], down[...], preferred_element_type=jnp.float32
        )
        for block in range(blocks):
            rows[half, pl.ds(block, count, stride=blocks), :] = made[
                :, block * LANES : (block + 1) * LANES
            ]
        target[...] = rows[half].astype(jnp.bfloat16)


def experts(arrived, partner, weights):
    features = weights[0][0].shape[1]
    count = arrived.shape[0] * arrived.shape[1] // features
    pieces, flat, units = [], [], 0
    for matrix, parts in enumerate(weights):
        row, column = 0, 0
        for part in parts:
            flat.append(part)
            pieces.append((matrix, row, column))
            column += part.shape[1]
            if column == features:
                row, column = row + part.shape[0], 0
        units = row
    vmem = pl.BlockSpec(memory_space=pltpu.VMEM)
    return pl.pallas_call(
        functools.partial(experts_kernel, pieces),
        out_shape=(jax.ShapeDtypeStruct(arrived.shape, jnp.bfloat16),) * 2,
        in_specs=[vmem] * 2 + [pl.BlockSpec(memory_space=pl.ANY)] * len(flat),
        out_specs=(vmem,) * 2,
        scratch_shapes=[pltpu.VMEM((units, features), jnp.bfloat16)] * 3
        + [
            pltpu.VMEM((2, *arrived.shape), jnp.float32),
            pltpu.VMEM((2 * count, features), jnp.bfloat16),
            pltpu.SemaphoreType.DMA((len(flat),)),
        ],
        compiler_params=pltpu.CompilerParams(vmem_limit_bytes=2 * VMEM_BYTES),
        cost_estimate=pl.CostEstimate(
            flops=12 * count * features * units,
            bytes_accessed=6 * units * features,
            transcendentals=2 * count * units,
        ),
        name="experts",
    )(arrived, partner, *flat)


def combine_kernel(returned, hidden, chosen_column, chosen_row, weight, out, rows, outputs):
    tokens, features = hidden.shape
    count = outputs.shape[0]
    blocks = features // LANES
    rows[...] = returned[...].astype(jnp.float32)
    for block in range(blocks):
        outputs[:, block * LANES : (block + 1) * LANES] = rows[
            pl.ds(block, count, stride=blocks), :
        ].astype(jnp.bfloat16)
    earlier = lax.broadcasted_iota(jnp.int32, (tokens, tokens), 1) < lax.broadcasted_iota(
        jnp.int32, (tokens, tokens), 0
    )
    same = (chosen_column[...] == chosen_row[...]) & earlier
    rank = jnp.sum(jnp.where(same, 1.0, 0.0), axis=1, keepdims=True)
    slot = slots(chosen_column[...], rank)
    pick = jnp.where(lax.broadcasted_iota(jnp.int32, (tokens, count), 1) == slot, 1.0, 0.0)
    picked = jnp.dot(pick.astype(jnp.bfloat16), outputs[...], preferred_element_type=jnp.float32)
    out[...] = (hidden[...].astype(jnp.float32) + weight[...] * picked).astype(jnp.bfloat16)


def combine(returned, hidden, chosen, weight):
    tokens, features = hidden.shape
    count = 64 * MOST
    vmem = pl.BlockSpec(memory_space=pltpu.VMEM)
    return pl.pallas_call(
        combine_kernel,
        out_shape=jax.ShapeDtypeStruct(hidden.shape, jnp.bfloat16),
        in_specs=[vmem] * 5,
        out_specs=vmem,
        scratch_shapes=[
            pltpu.VMEM(returned.shape, jnp.float32),
            pltpu.VMEM((count, features), jnp.bfloat16),
        ],
        compiler_params=pltpu.CompilerParams(vmem_limit_bytes=VMEM_BYTES),
        name="combine",
    )(returned, hidden, chosen, chosen.reshape(1, tokens), weight)


def after(value, *others):
    return lax.optimization_barrier((value, *others))[0]


def swapped(rows):
    return lax.ppermute(rows, "c", [(0, 1), (1, 0)])


def passed_along(block, by):
    return lax.ppermute(block, ("x", "y"), [(i, (i + by) % 16) for i in range(16)])


def per_device(
    queries,
    key_value,
    memory,
    memory_source,
    routing,
    router_weight,
    norm_gain,
    gate_matrix,
    up_matrix,
    down_matrix,
):
    features = queries.shape[1]
    kept = memory[0].transpose(1, 0, 2)
    near = passed_along(kept, 1)
    far = passed_along(kept, 2)
    moved = [
        lax.ppermute(matrix, ("x", "p"), spread_pairs())
        for matrix in (gate_matrix.T, up_matrix.T, down_matrix)
    ]
    placed = [lax.ppermute(matrix, ("x", "p"), lift_pairs()) for matrix in moved]
    hidden, packed = attend(
        memory_source,
        after(queries, *moved),
        key_value.transpose(1, 0, 2),
        near,
        far,
        routing,
        norm_gain.reshape(1, features),
    )
    packed, *placed = lax.optimization_barrier((packed, *placed))
    left = [lax.ppermute(matrix, "x", ring(1)) for matrix in placed]
    right = [lax.ppermute(matrix, "x", ring(-1)) for matrix in placed]
    middle = features // 2
    across = [
        [lax.ppermute(left[0], "x", ring(1))],
        [lax.ppermute(right[1], "x", ring(-1))],
        [
            lax.ppermute(left[2][:, :middle], "x", ring(1)),
            lax.ppermute(right[2][:, middle:], "x", ring(-1)),
        ],
    ]
    weights = [
        [own, before, behind, *beyond]
        for own, before, behind, beyond in zip(placed, left, right, across)
    ]
    chunks = packed.reshape(64, -1, LANES)
    arrived = lax.all_to_all(chunks, ("y", "s", "p"), 0, 0, tiled=True).reshape(packed.shape)
    partner = swapped(after(arrived, *sum(weights, [])))
    made, lent = experts(arrived, partner, weights)
    made = (made.astype(jnp.float32) + swapped(lent).astype(jnp.float32)).astype(jnp.bfloat16)
    returned = lax.all_to_all(made.reshape(chunks.shape), ("y", "s", "p"), 0, 0, tiled=True)
    return combine(returned.reshape(packed.shape), hidden, routing, router_weight)


def solution(mesh):
    every = ("x", "y", "s", "p", "c")
    fine = Mesh(np.asarray(mesh.devices).reshape(4, 4, 4, 4, 2), every)
    return jax.shard_map(
        per_device,
        mesh=fine,
        in_specs=(
            P(every, None),
            P(every, None, None),
            P(every, None, None, None),
            P(every),
            P(every, None),
            P(every, None),
            P(),
            P(None, every),
            P(None, every),
            P(every, None),
        ),
        out_specs=P(every, None),
        check_vma=False,
    )
```

```python
import functools
import math

import jax
import jax.numpy as jnp
import numpy as np
from jax import lax
from jax.experimental import pallas as pl
from jax.experimental.pallas import tpu as pltpu
from jax.sharding import Mesh
from jax.sharding import PartitionSpec as P

HEADS = 16
MOST = 3
LANES = 128
VMEM_BYTES = 16 * 1024 * 1024

PLACE = ((0, 2, 1, 3), (1, 3, 0, 2), (2, 0, 3, 1), (3, 1, 2, 0))


def spread_pairs():
    return [(PLACE[h][p] * 4 + p, h * 4 + p) for h in range(4) for p in range(1, 4)]


def lift_pairs():
    return [(h * 4 + p, h * 4 + PLACE[h][p]) for h in range(4) for p in range(4)]


def ring(by):
    return [(i, (i + by) % 4) for i in range(4)]


def slots(chosen, rank):
    x = jnp.right_shift(chosen, 4)
    y = jnp.bitwise_and(jnp.right_shift(chosen, 2), 3)
    segment = jnp.bitwise_and(chosen, 3)
    return (y * 16 + segment * 4 + x) * MOST + rank.astype(jnp.int32)


def attend_kernel(
    source,
    queries,
    own,
    near,
    far_off,
    chosen_column,
    chosen_row,
    gain,
    hidden_out,
    packed_out,
    recalled,
    normed,
    rows,
    sem,
):
    tokens, features = queries.shape

    def fetch(block):
        copy = pltpu.make_async_copy(block, recalled, sem)
        copy.start()
        copy.wait()

    @pl.when(source[0] == 0)
    def _():
        fetch(near)

    @pl.when(source[0] != 0)
    def _():
        fetch(far_off)

    later = lax.broadcasted_iota(jnp.int32, (tokens, tokens), 1) > lax.broadcasted_iota(
        jnp.int32, (tokens, tokens), 0
    )
    scale = 1.0 / math.sqrt(features // HEADS)
    transposed = (((1,), (1,)), ((), ()))
    squares = jnp.zeros((tokens, LANES), jnp.float32)
    for head in range(HEADS):
        at = slice(head * LANES, (head + 1) * LANES)
        query = queries[:, at]
        far = scale * lax.dot_general(
            query, recalled[0, :, at], transposed, preferred_element_type=jnp.float32
        )
        here = scale * lax.dot_general(
            query, own[0, :, at], transposed, preferred_element_type=jnp.float32
        )
        here = jnp.where(later, -1e30, here)
        top = jnp.max(jnp.maximum(far, here), axis=1, keepdims=True)
        far = jnp.exp(far - top)
        here = jnp.exp(here - top)
        share = 1.0 / jnp.sum(far + here, axis=1, keepdims=True)
        hidden = jnp.dot(
            (far * share).astype(jnp.bfloat16),
            recalled[1, :, at],
            preferred_element_type=jnp.float32,
        ) + jnp.dot(
            (here * share).astype(jnp.bfloat16), own[1, :, at], preferred_element_type=jnp.float32
        )
        hidden = hidden.astype(jnp.bfloat16)
        hidden_out[:, at] = hidden
        wide = hidden.astype(jnp.float32)
        squares += wide * wide
    mean = jnp.sum(squares, axis=1, keepdims=True) / features
    factor = lax.rsqrt(mean + 1e-6)
    for head in range(HEADS):
        at = slice(head * LANES, (head + 1) * LANES)
        normed[:, at] = (hidden_out[:, at].astype(jnp.float32) * factor * gain[:, at]).astype(
            jnp.bfloat16
        )
    same = (chosen_column[...] == chosen_row[...]) & later
    rank = jnp.sum(jnp.where(same, 1.0, 0.0), axis=0, keepdims=True)
    slot = slots(chosen_row[...], rank)
    count = rows.shape[0] // (features // LANES)
    spread = jnp.where(lax.broadcasted_iota(jnp.int32, (count, tokens), 0) == slot, 1.0, 0.0)
    spread = spread.astype(jnp.bfloat16)
    blocks = features // LANES
    packed = jnp.dot(spread, normed[...], preferred_element_type=jnp.float32)
    for block in range(blocks):
        rows[pl.ds(block, count, stride=blocks), :] = packed[:, block * LANES : (block + 1) * LANES]
    packed_out[...] = rows[...].astype(jnp.bfloat16)


def attend(source, queries, own, near, far, chosen, gain):
    tokens, features = queries.shape
    blocks = features // LANES
    count = 64 * MOST
    vmem = pl.BlockSpec(memory_space=pltpu.VMEM)
    anywhere = pl.BlockSpec(memory_space=pl.ANY)
    return pl.pallas_call(
        attend_kernel,
        out_shape=(
            jax.ShapeDtypeStruct((tokens, features), jnp.bfloat16),
            jax.ShapeDtypeStruct((count * blocks, LANES), jnp.bfloat16),
        ),
        in_specs=[pl.BlockSpec(memory_space=pltpu.SMEM)]
        + [vmem] * 2
        + [anywhere] * 2
        + [vmem] * 3,
        out_specs=(vmem, vmem),
        scratch_shapes=[
            pltpu.VMEM((2, tokens, features), jnp.bfloat16),
            pltpu.VMEM((tokens, features), jnp.bfloat16),
            pltpu.VMEM((count * blocks, LANES), jnp.float32),
            pltpu.SemaphoreType.DMA,
        ],
        compiler_params=pltpu.CompilerParams(vmem_limit_bytes=VMEM_BYTES),
        cost_estimate=pl.CostEstimate(
            flops=4 * tokens * 2 * tokens * features,
            bytes_accessed=10 * tokens * features,
            transcendentals=2 * HEADS * tokens * tokens,
        ),
        name="attend",
    )(source, queries, own, near, far, chosen, chosen.reshape(1, tokens), gain)


def experts_kernel(pieces, arrived, partner, *refs):
    sources = refs[: len(pieces)]
    out, lent, gate, up, down, rows, tokens, sems = refs[len(pieces) :]
    copies = ([], [], [])
    for number, (source, (matrix, row, column)) in enumerate(zip(sources, pieces)):
        units, width = source.shape
        target = (gate, up, down)[matrix].at[pl.ds(row, units), pl.ds(column, width)]
        copy = pltpu.make_async_copy(source, target, sems.at[number])
        copy.start()
        copies[matrix].append(copy)
    count, features = tokens.shape[0] // 2, tokens.shape[1]
    blocks = features // LANES
    for half, block_rows in enumerate((arrived, partner)):
        rows[half] = block_rows[...].astype(jnp.float32)
        for block in range(blocks):
            tokens[half * count : (half + 1) * count, block * LANES : (block + 1) * LANES] = rows[
                half, pl.ds(block, count, stride=blocks), :
            ].astype(jnp.bfloat16)
    for copy in copies[0] + copies[1]:
        copy.wait()
    transposed = (((1,), (1,)), ((), ()))
    gated = lax.dot_general(
        tokens[...], gate[...], transposed, preferred_element_type=jnp.float32
    )
    raised = lax.dot_general(tokens[...], up[...], transposed, preferred_element_type=jnp.float32)
    act = (gated / (1.0 + jnp.exp(-gated)) * raised).astype(jnp.bfloat16)
    for copy in copies[2]:
        copy.wait()
    for half, target in ((1, lent), (0, out)):
        made = jnp.dot(
            act[half * count : (half + 1) * count], down[...], preferred_element_type=jnp.float32
        )
        for block in range(blocks):
            rows[half, pl.ds(block, count, stride=blocks), :] = made[
                :, block * LANES : (block + 1) * LANES
            ]
        target[...] = rows[half].astype(jnp.bfloat16)


def experts(arrived, partner, weights):
    features = weights[0][0].shape[1]
    count = arrived.shape[0] * arrived.shape[1] // features
    pieces, flat, units = [], [], 0
    for matrix, parts in enumerate(weights):
        row, column = 0, 0
        for part in parts:
            flat.append(part)
            pieces.append((matrix, row, column))
            column += part.shape[1]
            if column == features:
                row, column = row + part.shape[0], 0
        units = row
    vmem = pl.BlockSpec(memory_space=pltpu.VMEM)
    return pl.pallas_call(
        functools.partial(experts_kernel, pieces),
        out_shape=(jax.ShapeDtypeStruct(arrived.shape, jnp.bfloat16),) * 2,
        in_specs=[vmem] * 2 + [pl.BlockSpec(memory_space=pl.ANY)] * len(flat),
        out_specs=(vmem,) * 2,
        scratch_shapes=[pltpu.VMEM((units, features), jnp.bfloat16)] * 3
        + [
            pltpu.VMEM((2, *arrived.shape), jnp.float32),
            pltpu.VMEM((2 * count, features), jnp.bfloat16),
            pltpu.SemaphoreType.DMA((len(flat),)),
        ],
        compiler_params=pltpu.CompilerParams(vmem_limit_bytes=56 * 1024 * 1024),
        cost_estimate=pl.CostEstimate(
            flops=12 * count * features * units,
            bytes_accessed=6 * units * features,
            transcendentals=2 * count * units,
        ),
        name="experts",
    )(arrived, partner, *flat)


def combine_kernel(returned, hidden, chosen_column, chosen_row, weight, out, rows, outputs):
    tokens, features = hidden.shape
    count = outputs.shape[0]
    blocks = features // LANES
    rows[...] = returned[...].astype(jnp.float32)
    for block in range(blocks):
        outputs[:, block * LANES : (block + 1) * LANES] = rows[
            pl.ds(block, count, stride=blocks), :
        ].astype(jnp.bfloat16)
    earlier = lax.broadcasted_iota(jnp.int32, (tokens, tokens), 1) < lax.broadcasted_iota(
        jnp.int32, (tokens, tokens), 0
    )
    same = (chosen_column[...] == chosen_row[...]) & earlier
    rank = jnp.sum(jnp.where(same, 1.0, 0.0), axis=1, keepdims=True)
    slot = slots(chosen_column[...], rank)
    pick = jnp.where(lax.broadcasted_iota(jnp.int32, (tokens, count), 1) == slot, 1.0, 0.0)
    picked = jnp.dot(pick.astype(jnp.bfloat16), outputs[...], preferred_element_type=jnp.float32)
    out[...] = (hidden[...].astype(jnp.float32) + weight[...] * picked).astype(jnp.bfloat16)


def combine(returned, hidden, chosen, weight):
    tokens, features = hidden.shape
    count = 64 * MOST
    vmem = pl.BlockSpec(memory_space=pltpu.VMEM)
    return pl.pallas_call(
        combine_kernel,
        out_shape=jax.ShapeDtypeStruct(hidden.shape, jnp.bfloat16),
        in_specs=[vmem] * 5,
        out_specs=vmem,
        scratch_shapes=[
            pltpu.VMEM(returned.shape, jnp.float32),
            pltpu.VMEM((count, features), jnp.bfloat16),
        ],
        compiler_params=pltpu.CompilerParams(vmem_limit_bytes=VMEM_BYTES),
        name="combine",
    )(returned, hidden, chosen, chosen.reshape(1, tokens), weight)


def after(value, *others):
    return lax.optimization_barrier((value, *others))[0]


def spread(matrix):
    moved = lax.ppermute(matrix, ("x", "p"), spread_pairs())
    return jnp.where(lax.axis_index("p") == 0, matrix, moved)


def swapped(rows):
    return lax.ppermute(rows, "c", [(0, 1), (1, 0)])


def passed_along(block, by):
    return lax.ppermute(block, ("x", "y"), [(i, (i + by) % 16) for i in range(16)])


def per_device(
    queries,
    key_value,
    memory,
    memory_source,
    routing,
    router_weight,
    norm_gain,
    gate_matrix,
    up_matrix,
    down_matrix,
):
    features = queries.shape[1]
    kept = memory[0].transpose(1, 0, 2)
    near = passed_along(kept, 1)
    far = passed_along(kept, 2)
    moved = [
        spread(after(matrix, near, far)) for matrix in (gate_matrix.T, up_matrix.T, down_matrix)
    ]
    placed = [lax.ppermute(matrix, ("x", "p"), lift_pairs()) for matrix in moved]
    hidden, packed = attend(
        memory_source,
        queries,
        key_value.transpose(1, 0, 2),
        near,
        far,
        routing,
        norm_gain.reshape(1, features),
    )
    left = [lax.ppermute(matrix, "x", ring(1)) for matrix in placed]
    right = [lax.ppermute(matrix, "x", ring(-1)) for matrix in placed]
    packed = after(packed, *placed, *left[:2], *right[:2])
    middle = features // 2
    across = [
        [lax.ppermute(left[0], "x", ring(1))],
        [lax.ppermute(right[1], "x", ring(-1))],
        [
            lax.ppermute(left[2][:, :middle], "x", ring(1)),
            lax.ppermute(right[2][:, middle:], "x", ring(-1)),
        ],
    ]
    weights = [
        [own, before, behind, *beyond]
        for own, before, behind, beyond in zip(placed, left, right, across)
    ]
    chunks = packed.reshape(64, -1, LANES)
    arrived = lax.all_to_all(chunks, ("y", "s", "p"), 0, 0, tiled=True).reshape(packed.shape)
    partner = swapped(after(arrived, *left, *right, *across[0], *across[1]))
    made, lent = experts(arrived, partner, weights)
    made = (made.astype(jnp.float32) + swapped(lent).astype(jnp.float32)).astype(jnp.bfloat16)
    returned = lax.all_to_all(made.reshape(chunks.shape), ("y", "s", "p"), 0, 0, tiled=True)
    return combine(returned.reshape(packed.shape), hidden, routing, router_weight)


def solution(mesh):
    every = ("x", "y", "s", "p", "c")
    fine = Mesh(np.asarray(mesh.devices).reshape(4, 4, 4, 4, 2), every)
    return jax.shard_map(
        per_device,
        mesh=fine,
        in_specs=(
            P(every, None),
            P(every, None, None),
            P(every, None, None, None),
            P(every),
            P(every, None),
            P(every, None),
            P(),
            P(None, every),
            P(None, every),
            P(every, None),
        ),
        out_specs=P(every, None),
        check_vma=False,
    )
```

```python
import functools
import math

import jax
import jax.numpy as jnp
import numpy as np
from jax import lax
from jax.experimental import pallas as pl
from jax.experimental.pallas import tpu as pltpu
from jax.sharding import Mesh
from jax.sharding import PartitionSpec as P

HEADS = 16
SLICES = 8
MOST = 3
LANES = 128
VMEM_BYTES = 52 * 1024 * 1024

PLACE = ((0, 2, 1, 3), (1, 3, 0, 2), (2, 0, 3, 1), (3, 1, 2, 0))


def spread_pairs():
    return [(PLACE[h][p] * 4 + p, h * 4 + p) for h in range(4) for p in range(1, 4)]


def lift_pairs():
    return [(h * 4 + p, h * 4 + PLACE[h][p]) for h in range(4) for p in range(4)]


def ring(by):
    return [(i, (i + by) % 4) for i in range(4)]


def slots(chosen, rank):
    x = jnp.right_shift(chosen, 4)
    y = jnp.bitwise_and(jnp.right_shift(chosen, 2), 3)
    segment = jnp.bitwise_and(chosen, 3)
    return (y * 16 + segment * 4 + x) * MOST + rank.astype(jnp.int32)


def attend_kernel(
    source,
    queries,
    own,
    near,
    far_off,
    chosen_column,
    chosen_row,
    gain,
    hidden_out,
    packed_out,
    recalled,
    normed,
    rows,
    sem,
):
    tokens, features = queries.shape

    def fetch(block):
        copy = pltpu.make_async_copy(block, recalled, sem)
        copy.start()
        copy.wait()

    @pl.when(source[0] == 0)
    def _():
        fetch(near)

    @pl.when(source[0] != 0)
    def _():
        fetch(far_off)

    later = lax.broadcasted_iota(jnp.int32, (tokens, tokens), 1) > lax.broadcasted_iota(
        jnp.int32, (tokens, tokens), 0
    )
    scale = 1.0 / math.sqrt(features // HEADS)
    transposed = (((1,), (1,)), ((), ()))
    squares = jnp.zeros((tokens, LANES), jnp.float32)
    for head in range(HEADS):
        at = slice(head * LANES, (head + 1) * LANES)
        query = queries[:, at]
        far = scale * lax.dot_general(
            query, recalled[0, :, at], transposed, preferred_element_type=jnp.float32
        )
        here = scale * lax.dot_general(
            query, own[0, :, at], transposed, preferred_element_type=jnp.float32
        )
        here = jnp.where(later, -1e30, here)
        top = jnp.max(jnp.maximum(far, here), axis=1, keepdims=True)
        far = jnp.exp(far - top)
        here = jnp.exp(here - top)
        share = 1.0 / jnp.sum(far + here, axis=1, keepdims=True)
        hidden = jnp.dot(
            (far * share).astype(jnp.bfloat16),
            recalled[1, :, at],
            preferred_element_type=jnp.float32,
        ) + jnp.dot(
            (here * share).astype(jnp.bfloat16), own[1, :, at], preferred_element_type=jnp.float32
        )
        hidden = hidden.astype(jnp.bfloat16)
        hidden_out[:, at] = hidden
        wide = hidden.astype(jnp.float32)
        squares += wide * wide
    mean = jnp.sum(squares, axis=1, keepdims=True) / features
    factor = lax.rsqrt(mean + 1e-6)
    for head in range(HEADS):
        at = slice(head * LANES, (head + 1) * LANES)
        normed[:, at] = (hidden_out[:, at].astype(jnp.float32) * factor * gain[:, at]).astype(
            jnp.bfloat16
        )
    same = (chosen_column[...] == chosen_row[...]) & later
    rank = jnp.sum(jnp.where(same, 1.0, 0.0), axis=0, keepdims=True)
    slot = slots(chosen_row[...], rank)
    count = rows.shape[0] // (features // LANES)
    spread = jnp.where(lax.broadcasted_iota(jnp.int32, (count, tokens), 0) == slot, 1.0, 0.0)
    spread = spread.astype(jnp.bfloat16)
    blocks = features // LANES
    packed = jnp.dot(spread, normed[...], preferred_element_type=jnp.float32)
    for block in range(blocks):
        rows[pl.ds(block, count, stride=blocks), :] = packed[:, block * LANES : (block + 1) * LANES]
    packed_out[...] = rows[...].astype(jnp.bfloat16)


def attend(source, queries, own, near, far, chosen, gain):
    tokens, features = queries.shape
    blocks = features // LANES
    count = 64 * MOST
    vmem = pl.BlockSpec(memory_space=pltpu.VMEM)
    anywhere = pl.BlockSpec(memory_space=pl.ANY)
    return pl.pallas_call(
        attend_kernel,
        out_shape=(
            jax.ShapeDtypeStruct((tokens, features), jnp.bfloat16),
            jax.ShapeDtypeStruct((count * blocks, LANES), jnp.bfloat16),
        ),
        in_specs=[pl.BlockSpec(memory_space=pltpu.SMEM)]
        + [vmem] * 2
        + [anywhere] * 2
        + [vmem] * 3,
        out_specs=(vmem, vmem),
        scratch_shapes=[
            pltpu.VMEM((2, tokens, features), jnp.bfloat16),
            pltpu.VMEM((tokens, features), jnp.bfloat16),
            pltpu.VMEM((count * blocks, LANES), jnp.float32),
            pltpu.SemaphoreType.DMA,
        ],
        compiler_params=pltpu.CompilerParams(vmem_limit_bytes=VMEM_BYTES),
        cost_estimate=pl.CostEstimate(
            flops=4 * tokens * 2 * tokens * features,
            bytes_accessed=10 * tokens * features,
            transcendentals=2 * HEADS * tokens * tokens,
        ),
        name="attend",
    )(source, queries, own, near, far, chosen, chosen.reshape(1, tokens), gain)


def experts_kernel(pieces, arrived, *refs):
    total = sum(len(half) for matrix in pieces for half in matrix)
    sources, (out, gate, up, down, rows, tokens, sems) = refs[:total], refs[total:]
    copies, number = [], 0
    for matrix, target in zip(pieces, (gate, up, down)):
        first = 0
        for half in matrix:
            group = []
            for size in half:
                group.append(
                    pltpu.make_async_copy(
                        sources[number], target.at[pl.ds(first, size)], sems.at[number]
                    )
                )
                first += size
                number += 1
            copies.append(group)
    for index in (0, 2, 1, 3, 4, 5):
        for copy in copies[index]:
            copy.start()
    count, features = tokens.shape
    blocks = features // LANES
    rows[...] = arrived[...].astype(jnp.float32)
    for block in range(blocks):
        tokens[:, block * LANES : (block + 1) * LANES] = rows[
            pl.ds(block, count, stride=blocks), :
        ].astype(jnp.bfloat16)
    transposed = (((1,), (1,)), ((), ()))
    middle = gate.shape[0] // 2
    acts = []
    for half in range(2):
        for copy in copies[half] + copies[2 + half]:
            copy.wait()
        at = slice(half * middle, (half + 1) * middle)
        gated = lax.dot_general(
            tokens[...], gate[at, :], transposed, preferred_element_type=jnp.float32
        )
        raised = lax.dot_general(
            tokens[...], up[at, :], transposed, preferred_element_type=jnp.float32
        )
        acts.append((gated / (1.0 + jnp.exp(-gated)) * raised).astype(jnp.bfloat16))
    for copy in copies[4] + copies[5]:
        copy.wait()
    made = jnp.dot(acts[0], down[:middle, :], preferred_element_type=jnp.float32) + jnp.dot(
        acts[1], down[middle:, :], preferred_element_type=jnp.float32
    )
    for block in range(blocks):
        rows[pl.ds(block, count, stride=blocks), :] = made[:, block * LANES : (block + 1) * LANES]
    out[...] = rows[...].astype(jnp.bfloat16)


def experts(arrived, weights):
    features = weights[0][0][0].shape[1]
    count = arrived.shape[0] * arrived.shape[1] // features
    pieces = [[[piece.shape[0] for piece in half] for half in matrix] for matrix in weights]
    units = sum(sum(half) for half in pieces[0])
    flat = [piece for matrix in weights for half in matrix for piece in half]
    vmem = pl.BlockSpec(memory_space=pltpu.VMEM)
    return pl.pallas_call(
        functools.partial(experts_kernel, pieces),
        out_shape=jax.ShapeDtypeStruct(arrived.shape, jnp.bfloat16),
        in_specs=[vmem] + [pl.BlockSpec(memory_space=pl.ANY)] * len(flat),
        out_specs=vmem,
        scratch_shapes=[pltpu.VMEM((units, features), jnp.bfloat16)] * 3
        + [
            pltpu.VMEM(arrived.shape, jnp.float32),
            pltpu.VMEM((count, features), jnp.bfloat16),
            pltpu.SemaphoreType.DMA((len(flat),)),
        ],
        compiler_params=pltpu.CompilerParams(vmem_limit_bytes=VMEM_BYTES),
        cost_estimate=pl.CostEstimate(
            flops=6 * count * features * units,
            bytes_accessed=6 * units * features,
            transcendentals=count * units,
        ),
        name="experts",
    )(arrived, *flat)


def combine_kernel(returned, hidden, chosen_column, chosen_row, weight, out, rows, outputs):
    tokens, features = hidden.shape
    count = outputs.shape[0]
    blocks = features // LANES
    rows[...] = returned[...].astype(jnp.float32)
    for block in range(blocks):
        outputs[:, block * LANES : (block + 1) * LANES] = rows[
            pl.ds(block, count, stride=blocks), :
        ].astype(jnp.bfloat16)
    earlier = lax.broadcasted_iota(jnp.int32, (tokens, tokens), 1) < lax.broadcasted_iota(
        jnp.int32, (tokens, tokens), 0
    )
    same = (chosen_column[...] == chosen_row[...]) & earlier
    rank = jnp.sum(jnp.where(same, 1.0, 0.0), axis=1, keepdims=True)
    slot = slots(chosen_column[...], rank)
    pick = jnp.where(lax.broadcasted_iota(jnp.int32, (tokens, count), 1) == slot, 1.0, 0.0)
    picked = jnp.dot(pick.astype(jnp.bfloat16), outputs[...], preferred_element_type=jnp.float32)
    out[...] = (hidden[...].astype(jnp.float32) + weight[...] * picked).astype(jnp.bfloat16)


def combine(returned, hidden, chosen, weight):
    tokens, features = hidden.shape
    count = 64 * MOST
    vmem = pl.BlockSpec(memory_space=pltpu.VMEM)
    return pl.pallas_call(
        combine_kernel,
        out_shape=jax.ShapeDtypeStruct(hidden.shape, jnp.bfloat16),
        in_specs=[vmem] * 5,
        out_specs=vmem,
        scratch_shapes=[
            pltpu.VMEM(returned.shape, jnp.float32),
            pltpu.VMEM((count, features), jnp.bfloat16),
        ],
        compiler_params=pltpu.CompilerParams(vmem_limit_bytes=VMEM_BYTES),
        name="combine",
    )(returned, hidden, chosen, chosen.reshape(1, tokens), weight)


def gathered(matrix, which):
    moved = lax.ppermute(matrix, ("x", "p"), spread_pairs())
    moved = jnp.where(lax.axis_index("p") == 0, matrix, moved)
    own = lax.ppermute(moved, ("x", "p"), lift_pairs())
    left = lax.ppermute(own, "x", ring(1))
    right = lax.ppermute(own, "x", ring(-1))
    if which == 0:
        far = [lax.ppermute(left, "x", ring(1))]
    elif which == 1:
        far = [lax.ppermute(right, "x", ring(-1))]
    else:
        cut = 96
        far = [lax.ppermute(left[:cut], "x", ring(1)), lax.ppermute(right[cut:], "x", ring(-1))]
    other = lambda piece: lax.ppermute(piece, "c", [(0, 1), (1, 0)])
    first, second = [own, left], [right, *far]
    return [first + [other(piece) for piece in first], second + [other(piece) for piece in second]]


def passed_along(block, by):
    return lax.ppermute(block, ("x", "y"), [(i, (i + by) % 16) for i in range(16)])


def per_device(
    queries,
    key_value,
    memory,
    memory_source,
    routing,
    router_weight,
    norm_gain,
    gate_matrix,
    up_matrix,
    down_matrix,
):
    features = queries.shape[1]
    kept = memory[0].transpose(1, 0, 2)
    near = passed_along(kept, 1)
    far = passed_along(kept, 2)
    weights = [
        gathered(matrix, which)
        for which, matrix in enumerate((gate_matrix.T, up_matrix.T, down_matrix))
    ]
    own = key_value.transpose(1, 0, 2)
    hidden, packed = attend(
        memory_source, queries, own, near, far, routing, norm_gain.reshape(1, features)
    )
    chunks = packed.reshape(64, -1, LANES)
    arrived = lax.all_to_all(chunks, ("y", "s", "p"), 0, 0, tiled=True)
    made = experts(arrived.reshape(packed.shape), weights)
    returned = lax.all_to_all(made.reshape(chunks.shape), ("y", "s", "p"), 0, 0, tiled=True)
    return combine(returned.reshape(packed.shape), hidden, routing, router_weight)


def solution(mesh):
    every = ("x", "y", "s", "p", "c")
    fine = Mesh(np.asarray(mesh.devices).reshape(4, 4, 4, 4, 2), every)
    return jax.shard_map(
        per_device,
        mesh=fine,
        in_specs=(
            P(every, None),
            P(every, None, None),
            P(every, None, None, None),
            P(every),
            P(every, None),
            P(every, None),
            P(),
            P(None, every),
            P(None, every),
            P(every, None),
        ),
        out_specs=P(every, None),
        check_vma=False,
    )
```
